256 devices in a mesh: expert: 32 (over y, x, core), tensor: 8 (over z).
Axes of the slice: x: 4, y: 4, z: 8, core: 2. Of those that a mesh axis runs over, the one named last changes fastest.
Arguments:
- tokens: bfloat16 [16384, 4096], P('expert', 'tensor'), may hold values from -36 to 36
- expert_ids: int32 [16384, 1], P('expert'), may hold values from 0 to 63; in each aligned block of 512 rows (0 to 511, 512 to 1023, ...) at most 16 rows name the same one
- gates: float32 [16384, 1], P('expert'), may hold values from 0.25 to 1
- expert_in: bfloat16 [64, 4096, 2048], P('expert', 'tensor'), may hold values from -0.09375 to 0.09375
- expert_out: bfloat16 [64, 2048, 4096], P('expert', None, 'tensor'), may hold values from -0.125 to 0.125
- norm_gain: float32 [4096], replicated, may hold values from 0.5 to 2
- up_weight: bfloat16 [4096, 8192], P('expert', 'tensor'), may hold values from -0.09375 to 0.09375
- down_weight: bfloat16 [4096, 8192], P('expert', 'tensor'), may hold values from -0.0625 to 0.0625
Outputs:
- layer_output: bfloat16 [16384, 4096], P('expert', 'tensor')
The draws below stay inside these ranges and needn't reach their ends.
Inputs may be any that keep to these rules, and one draw needn't show every extreme that they name: `expert_ids`: among the 512 tokens of one block, at most 16 carry the same expert id; in some blocks one id is carried by exactly 16 tokens.
All inputs are finite; a program needn't handle non-finite values.
Results may differ from the reference program's by a relative error of at most 0.015.
Values may be sent and summed in bfloat16 or wider, within the bound.
No kernel may reach another device: no remote copies, remote signals or barrier semaphores. Data moves between devices by JAX's collectives and lax.ppermute only.
A program may use at most 128 MiB of HBM per device.

```python
import math
import jax
import jax.numpy as jnp
import numpy as np
from jax import lax

D = 4096
EXP_HIDDEN = 2048
FFN_HIDDEN = 8192
TOK_DEV = 512
EXPERTS = 64
TOKENS = 16384
CAP = 16
N_EXPERT = 32
N_TENSOR = 8


def draw_tokens(key, part):
    key = jax.random.fold_in(key, 11)
    row_key, column_key, base_key = jax.random.split(key, 3)
    row_scale = jnp.exp(jax.random.uniform(row_key, (TOKENS, 1), jnp.float32, math.log(0.3), math.log(3.0)))
    column_scale = jnp.exp(jax.random.uniform(column_key, (1, D), jnp.float32, math.log(0.3), math.log(3.0)))
    base = jnp.clip(jax.random.normal(base_key, (TOKENS, D), jnp.float32), -4.0, 4.0)
    return (base * row_scale * column_scale).astype(jnp.bfloat16)


def block_scale(rng, shape, cuts, low, top_value):
    gain = 1.0
    for dim, shards_of in cuts:
        heights = jax.random.uniform(jax.random.fold_in(jax.random.fold_in(rng, 6), dim), (shards_of,), jnp.float32, low / len(cuts), top_value / len(cuts))
        gain = gain * jnp.repeat(jnp.exp(heights), shape[dim] // shards_of).reshape((-1,) + (1,) * (len(shape) - 1 - dim))
    return gain


def deal_out(own_key, own, number, rows, number_of, top, most, slope):
    sequence = jax.random.permutation(own_key, number_of)
    packed, common = load_shares(number_of, rows * top, most, slope, True), load_shares(number_of, rows * top, most, slope, False)
    places = jnp.arange(number_of)

    def named(lengths, rotation):
        used = int((lengths > 0).sum())
        fixed = max(1, used // 4)
        shifted = fixed + (places - fixed + rotation * (used - fixed)) % max(1, number_of - fixed)
        return jnp.zeros((number_of,), jnp.int32).at[sequence[jnp.where(places < fixed, places, shifted)]].set(jnp.asarray(lengths, jnp.int32))

    lengths = jnp.where(number % 4 == 0, named(packed, number // 4), named(common, number - number // 4 - 1))
    mixed = jax.random.permutation(jax.random.fold_in(own, 3), number_of)
    donor, sink = mixed[0:number_of // 2 * 2:2], mixed[1:number_of // 2 * 2:2]
    room = jnp.minimum(lengths[donor] - 1, most - lengths[sink]) // 2
    room = jnp.where((donor == sequence[0]) | (sink == sequence[0]) | (lengths[sink] == 0), 0, jnp.maximum(room, 0))
    shifted = jax.random.randint(jax.random.fold_in(own, 4), (number_of // 2,), 0, 1 << 20) % (room + 1)
    lengths = lengths.at[donor].add(-shifted).at[sink].add(shifted)
    labels = jnp.searchsorted(jnp.cumsum(lengths), jnp.arange(rows * top), side="right").astype(jnp.int32)
    listing = labels.reshape(top, rows).T
    listing = listing[jax.random.permutation(jax.random.fold_in(own, 1), rows)]
    rotation = jax.random.randint(jax.random.fold_in(own, 2), (rows, 1), 0, top)
    return jnp.take_along_axis(listing, (jnp.arange(top)[None, :] + rotation) % top, axis=1)


def load_shares(count, total, most, slope, full):
    weights = [(1 << 20) // math.isqrt(grade ** slope) + 1 for grade in range(1, count + 1)]
    largest = most if full else min(most, max(-(-total // count), total * weights[0] // sum(weights)))
    least = 1 if total - largest >= count - 1 else 0
    holding, spare = [largest] + [least] * (count - 1), total - largest - least * (count - 1)
    while spare > 0:
        free = [i for i in range(1, count) if holding[i] < largest] or [i for i in range(1, count) if holding[i] < most]
        mass, budget = sum([weights[i] for i in free]), spare
        for i in free:
            addition = min(most - holding[i], max(1, budget * weights[i] // mass), spare)
            holding[i] = holding[i] + addition
            spare = spare - addition
    return np.array(holding)


def noise(rng, extent, width, limit, cuts=(), kind=jnp.bfloat16):
    values = jax.random.normal(rng, extent, jnp.float32) * width
    if len(cuts) > 0:
        values = block_scale(rng, extent, cuts, -0.22, 0.18) * values
    return jnp.clip(values, min=-limit, max=limit).astype(kind)


def setup_inputs(seed: int = 0) -> dict:
    key_of = jax.random.split(jax.random.key(seed), 9)
    tokens = draw_tokens(jax.random.fold_in(key_of[8], 71), 0)
    expert_ids_keys = jax.random.split(jax.random.fold_in(key_of[1], 1), TOKENS // TOK_DEV)
    expert_ids_turns = jax.random.permutation(jax.random.fold_in(key_of[1], 3), TOKENS // TOK_DEV)
    expert_ids = jax.vmap(lambda own, number: deal_out(jax.random.fold_in(key_of[1], 2), own, number, TOK_DEV, EXPERTS, 1, CAP, 2))(expert_ids_keys, expert_ids_turns).reshape((TOKENS, 1))
    gates = jnp.clip(0.25 + 0.75 * jax.random.uniform(key_of[2], (TOKENS, 1), jnp.float32) ** block_scale(key_of[2], (TOKENS, 1), ((0, 32),), -0.2, 0.2), 0.25, 1.0)
    expert_in = noise(key_of[3], (EXPERTS, D, EXP_HIDDEN), D ** -0.5, 0.09375, ((0, 32), (1, 8)))
    expert_out = noise(key_of[4], (EXPERTS, EXP_HIDDEN, D), EXP_HIDDEN ** -0.5, 0.125, ((0, 32), (2, 8)))
    norm_gain = jnp.clip(jnp.exp(jax.random.uniform(key_of[5], (D,), jnp.float32, math.log(0.5), math.log(2.0))), 0.5, 2.0)
    up_weight = noise(key_of[6], (D, FFN_HIDDEN), D ** -0.5, 0.09375, ((0, 32), (1, 8)))
    down_weight = noise(key_of[7], (D, FFN_HIDDEN), FFN_HIDDEN ** -0.5, 0.0625, ((0, 32), (1, 8)))
    return dict(tokens=tokens, expert_ids=expert_ids, gates=gates, expert_in=expert_in, expert_out=expert_out, norm_gain=norm_gain, up_weight=up_weight, down_weight=down_weight)


def slot_table(expert_col, experts, capacity):
    expert = expert_col[:, 0]
    onehot = (expert[:, None] == jnp.arange(experts, dtype=jnp.int32)[None, :]).astype(jnp.int32)
    before = jnp.cumsum(onehot, axis=0) - onehot
    position = lax.optimization_barrier(jnp.sum(before * onehot, axis=1))
    slot_index = expert * capacity + position
    selector = jnp.arange(experts * capacity, dtype=jnp.int32)[:, None] == slot_index[None, :]
    return selector.astype(jnp.bfloat16)

def reference(tokens, expert_ids, gates, expert_in, expert_out, norm_gain, up_weight, down_weight):
    blocks = tokens.reshape(N_EXPERT, TOK_DEV, D)
    id_blocks = expert_ids.reshape(N_EXPERT, TOK_DEV, 1)
    gate_blocks = gates.reshape(N_EXPERT, TOK_DEV, 1)

    def dispatch_block(operands):
        token_rows, id_rows = operands
        selector = slot_table(id_rows, EXPERTS, CAP)
        return jnp.dot(selector, token_rows, preferred_element_type=jnp.float32).astype(jnp.bfloat16)
    outgoing = lax.map(dispatch_block, (blocks, id_blocks))
    by_expert = outgoing.reshape(N_EXPERT, EXPERTS, CAP, D).transpose(1, 0, 2, 3).reshape(EXPERTS, N_EXPERT * CAP, D)

    def expert_apply(operands):
        token_rows, weight_in, weight_out = operands
        left_side = token_rows.reshape(-1, N_TENSOR, D // N_TENSOR).astype(jnp.float32)
        right_side = weight_in.reshape(N_TENSOR, D // N_TENSOR, EXP_HIDDEN).astype(jnp.float32)
        partials = jnp.einsum('rtd,tdh->trh', left_side, right_side)
        partials = lax.optimization_barrier(partials.astype(jnp.bfloat16)).astype(jnp.float32)
        hidden = lax.optimization_barrier(jnp.sum(partials, axis=0))
        active = jax.nn.relu(hidden).astype(jnp.bfloat16)
        return jnp.dot(active, weight_out, preferred_element_type=jnp.float32).astype(jnp.bfloat16)
    results = lax.map(expert_apply, (by_expert, expert_in, expert_out))
    returned_all = results.reshape(EXPERTS, N_EXPERT, CAP, D).transpose(1, 0, 2, 3).reshape(N_EXPERT, EXPERTS * CAP, D)

    def combine(operands):
        token_rows, id_rows, gate_col, returned = operands
        selector = slot_table(id_rows, EXPERTS, CAP)
        routed = lax.dot_general(selector, returned, (((0,), (0,)), ((), ())), preferred_element_type=jnp.float32)
        return (token_rows.astype(jnp.float32) + gate_col * routed).astype(jnp.bfloat16)
    mixed = lax.map(combine, (blocks, id_blocks, gate_blocks, returned_all)).reshape(TOKENS, D)
    mixed_f32 = mixed.astype(jnp.float32)
    mean_square = lax.optimization_barrier(jnp.mean(mixed_f32 * mixed_f32, axis=1, keepdims=True))
    normed = (mixed_f32 * lax.rsqrt(mean_square + 1e-06) * norm_gain).astype(jnp.bfloat16)
    ffn_hidden = jnp.dot(normed, up_weight, preferred_element_type=jnp.float32)
    ffn_active = jax.nn.gelu(ffn_hidden, approximate=True).astype(jnp.bfloat16)
    share_width = FFN_HIDDEN // N_TENSOR
    summed = jnp.zeros((TOKENS, D), jnp.float32)
    for shard_index in range(N_TENSOR):
        lower_unit = shard_index * share_width
        block_out = lax.dot_general(ffn_active[:, lower_unit:lower_unit + share_width], down_weight[:, lower_unit:lower_unit + share_width], (((1,), (1,)), ((), ())), preferred_element_type=jnp.float32)
        summed = summed + lax.optimization_barrier(block_out.astype(jnp.bfloat16)).astype(jnp.float32)
    return (mixed_f32 + summed).astype(jnp.bfloat16)
```

```python
import jax
import jax.numpy as jnp
from jax import lax
from jax.sharding import PartitionSpec as P

EXP_DEV = 2


def slot_table(expert_col, experts, capacity):
    expert = expert_col[:, 0]
    count = expert.shape[0]
    order = jnp.arange(count, dtype=jnp.int32)
    same = (expert[:, None] == expert[None, :]) & (order[None, :] < order[:, None])
    position = jnp.sum(same.astype(jnp.int32), axis=1)
    slot_index = expert * capacity + position
    selector = jnp.arange(experts * capacity, dtype=jnp.int32)[:, None] == slot_index[None, :]
    return selector.astype(jnp.bfloat16)


def trade(buffer):
    result = lax.all_to_all(buffer, "expert", split_axis=0, concat_axis=0, tiled=True)
    return result


def gather_rows(weight, combine, start_value):
    return combine(start_value, lax.all_gather(weight, "expert", axis=0, tiled=True), jnp.int32(0))


def shards(tokens, expert_ids, gates, expert_in, expert_out, norm_gain, up_weight, down_weight):
    token_count = tokens.shape[0]
    local_width = tokens.shape[1]
    groups = lax.axis_size("expert")
    experts = EXP_DEV * groups
    capacity = 2 * token_count // experts
    selector = slot_table(expert_ids, experts, capacity)
    outgoing = jnp.dot(selector, tokens, preferred_element_type=jnp.float32).astype(jnp.bfloat16)
    outgoing = outgoing.reshape(groups, EXP_DEV, capacity, local_width)
    arrived = trade(outgoing)
    partial_value = jnp.einsum(
        "sjcd,jdh->sjch", arrived, expert_in, preferred_element_type=jnp.float32
    )
    summed = lax.psum(partial_value.astype(jnp.bfloat16), "tensor").astype(jnp.float32)
    active = jax.nn.relu(summed).astype(jnp.bfloat16)
    produced = jnp.einsum(
        "sjch,jhd->sjcd", active, expert_out, preferred_element_type=jnp.float32
    ).astype(jnp.bfloat16)
    returned = trade(produced).reshape(experts * capacity, local_width)
    routed = lax.dot_general(
        selector, returned, (((0,), (0,)), ((), ())), preferred_element_type=jnp.float32
    )
    mixed = (tokens.astype(jnp.float32) + gates * routed).astype(jnp.bfloat16)
    whole = lax.all_gather(mixed, "tensor", axis=1, tiled=True)
    whole_f32 = whole.astype(jnp.float32)
    mean_square = jnp.mean(whole_f32 * whole_f32, axis=1, keepdims=True)
    normed = (whole_f32 * lax.rsqrt(mean_square + 1e-06) * norm_gain).astype(jnp.bfloat16)

    def add_up(carry, piece, start):
        return jnp.dot(normed, piece, preferred_element_type=jnp.float32)

    ffn_hidden = gather_rows(
        up_weight, add_up, jnp.zeros((token_count, up_weight.shape[1]), jnp.float32)
    )
    ffn_active = jax.nn.gelu(ffn_hidden, approximate=True).astype(jnp.bfloat16)

    def add_down(carry, piece, start):
        contribution = lax.dot_general(
            ffn_active, piece, (((1,), (1,)), ((), ())), preferred_element_type=jnp.float32
        )
        return contribution

    outputs = gather_rows(
        down_weight, add_down, jnp.zeros((token_count, whole.shape[1]), jnp.float32)
    )
    summed_out = lax.psum_scatter(
        outputs.astype(jnp.bfloat16), "tensor", scatter_dimension=1, tiled=True
    ).astype(jnp.float32)
    return (mixed.astype(jnp.float32) + summed_out).astype(jnp.bfloat16)


def solution(mesh):
    return jax.shard_map(
        shards,
        mesh=mesh,
        in_specs=(
            P("expert", "tensor"),
            P("expert", None),
            P("expert", None),
            P("expert", "tensor", None),
            P("expert", None, "tensor"),
            P(),
            P("expert", "tensor"),
            P("expert", "tensor"),
        ),
        out_specs=P("expert", "tensor"),
        check_vma=False,
    )
```

```python
import jax
import jax.numpy as jnp
from jax import lax
from jax.sharding import PartitionSpec as P

EXP_DEV = 2
F32 = jnp.float32
BF16 = jnp.bfloat16


def slot_rows(expert_col):
    expert = expert_col[:, 0]
    order = jnp.arange(expert.shape[0], dtype=jnp.int32)
    same = (expert[:, None] == expert[None, :]) & (order[None, :] < order[:, None])
    position = jnp.sum(same.astype(jnp.int32), axis=1)
    return expert, position


def trade(buffer):
    return lax.all_to_all(buffer, "expert", split_axis=0, concat_axis=0, tiled=True)


def hop(value, shift):
    n = lax.axis_size("tensor")
    return lax.ppermute(value, "tensor", [(i, (i + shift) % n) for i in range(n)])


def ring_sum(chunk, rights):
    n = lax.axis_size("tensor")
    me = lax.axis_index("tensor")
    flows = []
    for shift, hops in ((1, rights), (-1, n - 1 - rights)):
        total = chunk((me + shift * hops) % n)
        for k in range(1, hops + 1):
            total = hop(total, shift).astype(F32)
            if k < hops:
                rest = chunk((me + shift * (hops - k)) % n).astype(F32)
                total = (total + rest).astype(BF16)
        flows.append(total)
    return flows[0] + flows[1] + chunk(me).astype(F32)


def ring_pieces(own, rights):
    n = lax.axis_size("tensor")
    me = lax.axis_index("tensor")
    pieces = [(me, own)]
    right = left = own
    for k in range(1, n):
        if k <= rights:
            right = hop(right, 1)
            pieces.append(((me - k) % n, right))
        if k <= n - 1 - rights:
            left = hop(left, -1)
            pieces.append(((me + k) % n, left))
    return pieces


def shards(tokens, expert_ids, gates, expert_in, expert_out, norm_gain, up_weight, down_weight):
    token_count, local_width = tokens.shape
    groups = lax.axis_size("expert")
    parts = lax.axis_size("tensor")
    experts = EXP_DEV * groups
    capacity = 2 * token_count // experts
    rows = groups * capacity
    expert, position = slot_rows(expert_ids)

    up_full = lax.all_gather(up_weight, "expert", axis=0, tiled=True)
    down_full = lax.all_gather(down_weight, "expert", axis=0, tiled=True)

    routed = jnp.zeros((token_count, local_width), F32)
    for j in range(EXP_DEV):
        row = jnp.where(expert % EXP_DEV == j, (expert // EXP_DEV) * capacity + position, -1)
        selector = (jnp.arange(rows, dtype=jnp.int32)[:, None] == row[None, :]).astype(BF16)
        outgoing = jnp.dot(selector, tokens, preferred_element_type=F32).astype(BF16)
        arrived = trade(outgoing.reshape(groups, capacity, local_width)).reshape(rows, local_width)
        partial = jnp.dot(arrived, expert_in[j], preferred_element_type=F32).astype(BF16)
        step = rows // parts

        def partial_rows(index):
            return lax.dynamic_slice_in_dim(partial, index * step, step, axis=0)

        rights = parts // 2 - j
        hidden = ring_sum(partial_rows, rights)
        own = jax.nn.relu(hidden).astype(BF16)
        active = jnp.zeros((rows, own.shape[1]), BF16)
        for index, piece in ring_pieces(own, rights):
            active = lax.dynamic_update_slice_in_dim(active, piece, index * step, axis=0)
        produced = jnp.dot(active, expert_out[j], preferred_element_type=F32).astype(BF16)
        returned = trade(produced.reshape(groups, capacity, local_width)).reshape(rows, local_width)
        routed = routed + lax.dot_general(
            selector, returned, (((0,), (0,)), ((), ())), preferred_element_type=F32
        )
    mixed = (tokens.astype(F32) + gates * routed).astype(BF16)

    outputs = []
    half = token_count // 2
    for h in range(2):
        rights = parts // 2 - h
        own = mixed[h * half : (h + 1) * half]
        hidden = jnp.zeros((half, up_full.shape[1]), F32)
        squares = jnp.zeros((half, 1), F32)
        for index, piece in ring_pieces(own, rights):
            wide = piece.astype(F32)
            squares = squares + jnp.sum(wide * wide, axis=1, keepdims=True)
            gain = lax.dynamic_slice_in_dim(norm_gain, index * local_width, local_width, axis=0)
            weight = lax.dynamic_slice_in_dim(up_full, index * local_width, local_width, axis=0)
            hidden = hidden + jnp.dot(
                (wide * gain).astype(BF16), weight, preferred_element_type=F32
            )
        scale = lax.rsqrt(squares / (parts * local_width) + 1e-06)
        ffn_active = jax.nn.gelu(hidden * scale, approximate=True).astype(BF16)

        def down_rows(index):
            weight = lax.dynamic_slice_in_dim(down_full, index * local_width, local_width, axis=0)
            return lax.dot_general(
                ffn_active, weight, (((1,), (1,)), ((), ())), preferred_element_type=F32
            ).astype(BF16)

        outputs.append((own.astype(F32) + ring_sum(down_rows, rights)).astype(BF16))
    return jnp.concatenate(outputs, axis=0)


def solution(mesh):
    return jax.shard_map(
        shards,
        mesh=mesh,
        in_specs=(
            P("expert", "tensor"),
            P("expert", None),
            P("expert", None),
            P("expert", "tensor", None),
            P("expert", None, "tensor"),
            P(),
            P("expert", "tensor"),
            P("expert", "tensor"),
        ),
        out_specs=P("expert", "tensor"),
        check_vma=False,
    )
```

```python
import jax
import jax.numpy as jnp
from jax import lax
from jax.sharding import PartitionSpec as P

EXP_DEV = 2
RING_SHARE = 10
F32 = jnp.float32
BF16 = jnp.bfloat16


def slot_rows(expert_col):
    expert = expert_col[:, 0]
    order = jnp.arange(expert.shape[0], dtype=jnp.int32)
    same = (expert[:, None] == expert[None, :]) & (order[None, :] < order[:, None])
    position = jnp.sum(same.astype(jnp.int32), axis=1)
    return expert, position


def trade(buffer):
    return lax.all_to_all(buffer, "expert", split_axis=0, concat_axis=0, tiled=True)


def hop(value, shift):
    n = lax.axis_size("tensor")
    return lax.ppermute(value, "tensor", [(i, (i + shift) % n) for i in range(n)])


def ring_sum(chunk, rights, ties=None):
    n = lax.axis_size("tensor")
    me = lax.axis_index("tensor")
    ways = ((1, rights), (-1, n - 1 - rights))
    flows = [chunk((me + shift * hops) % n) for shift, hops in ways]
    marks = {}
    for k in range(1, max(hops for _, hops in ways) + 1):
        for i, (shift, hops) in enumerate(ways):
            if k <= hops:
                flows[i] = hop(flows[i], shift)
        marks[k] = flows[0]
        if ties and k in ties:
            flows[0], flows[1], *_ = lax.optimization_barrier((flows[0], flows[1], *ties[k]))
        for i, (shift, hops) in enumerate(ways):
            if k < hops:
                rest = chunk((me + shift * (hops - k)) % n).astype(F32)
                flows[i] = (flows[i].astype(F32) + rest).astype(BF16)
    return flows[0].astype(F32) + flows[1].astype(F32) + chunk(me).astype(F32), marks


def ring_pieces(own, rights):
    n = lax.axis_size("tensor")
    me = lax.axis_index("tensor")
    pieces = [(me, own)]
    right = left = own
    for k in range(1, n):
        if k <= rights:
            right = hop(right, 1)
            pieces.append(((me - k) % n, right))
        if k <= n - 1 - rights:
            left = hop(left, -1)
            pieces.append(((me + k) % n, left))
    return pieces


def shards(tokens, expert_ids, gates, expert_in, expert_out, norm_gain, up_weight, down_weight):
    token_count, local_width = tokens.shape
    groups = lax.axis_size("expert")
    parts = lax.axis_size("tensor")
    experts = EXP_DEV * groups
    capacity = 2 * token_count // experts
    rows = groups * capacity
    expert, position = slot_rows(expert_ids)

    pairs = [[2 * i + c for i in range(groups // 2)] for c in range(2)]
    swap = [(i, i ^ 1) for i in range(groups)]
    core = lax.axis_index("expert") % 2

    mine = jnp.where(core == 0, up_weight, down_weight)
    other = lax.ppermute(jnp.where(core == 0, down_weight, up_weight), "expert", swap)
    unit = jnp.concatenate(
        [jnp.where(core == 0, mine, other), jnp.where(core == 0, other, mine)], axis=0
    )
    gathered = lax.all_gather(unit, "expert", axis=0, tiled=True, axis_index_groups=pairs)

    step = rows // parts
    rights = parts // 2
    selectors = []
    arrivals = []
    for j in range(EXP_DEV):
        row = jnp.where(expert % EXP_DEV == j, (expert // EXP_DEV) * capacity + position, -1)
        selector = (jnp.arange(rows, dtype=jnp.int32)[:, None] == row[None, :]).astype(BF16)
        outgoing = jnp.dot(selector, tokens, preferred_element_type=F32).astype(BF16)
        if j == 0:
            outgoing, unit = lax.optimization_barrier((outgoing, unit))
        selectors.append(selector)
        arrivals.append(
            trade(outgoing.reshape(groups, capacity, local_width)).reshape(rows, local_width)
        )

    def hidden_rows(arrived, weight):
        partial = jnp.dot(arrived, weight, preferred_element_type=F32).astype(BF16)
        return lambda index: lax.dynamic_slice_in_dim(partial, index * step, step, axis=0)

    sum_first, marks = ring_sum(
        hidden_rows(arrivals[0], expert_in[0]), rights, {2: arrivals[1:]}
    )
    own_first = jax.nn.relu(sum_first).astype(BF16)
    sum_second, _ = ring_sum(
        hidden_rows(arrivals[1], expert_in[1]), rights, {1: [marks[3]], 2: [own_first, gathered]}
    )
    owns = [own_first, jax.nn.relu(sum_second).astype(BF16)]

    active_first = lax.all_gather(owns[0], "tensor", axis=0, tiled=True)
    pieces = ring_pieces(owns[1], rights)
    late = 2 * rights - 2
    active_first, tied = lax.optimization_barrier((active_first, pieces[late][1]))
    pieces[late] = (pieces[late][0], tied)
    active_second = jnp.zeros((rows, owns[1].shape[1]), BF16)
    for index, piece in pieces:
        active_second = lax.dynamic_update_slice_in_dim(active_second, piece, index * step, axis=0)

    routed = jnp.zeros((token_count, local_width), F32)
    for j, active in enumerate((active_first, active_second)):
        produced = jnp.dot(active, expert_out[j], preferred_element_type=F32).astype(BF16)
        returned = trade(produced.reshape(groups, capacity, local_width)).reshape(rows, local_width)
        routed = routed + lax.dot_general(
            selectors[j], returned, (((0,), (0,)), ((), ())), preferred_element_type=F32
        )

    swapped = lax.ppermute(gathered, "expert", swap)
    up_full = jnp.where(core == 0, gathered, swapped)
    down_full = jnp.where(core == 0, swapped, gathered)
    routed, up_full, down_full = lax.optimization_barrier((routed, up_full, down_full))
    mixed = (tokens.astype(F32) + gates * routed).astype(BF16)

    def active_units(whole):
        wide = whole.astype(F32)
        mean_square = jnp.mean(wide * wide, axis=1, keepdims=True)
        normed = (wide * lax.rsqrt(mean_square + 1e-06) * norm_gain).astype(BF16)
        hidden = jnp.dot(normed, up_full, preferred_element_type=F32)
        return jax.nn.gelu(hidden, approximate=True).astype(BF16)

    def project_down(units, weight):
        return lax.dot_general(
            units, weight, (((1,), (1,)), ((), ())), preferred_element_type=F32
        ).astype(BF16)

    cut = token_count * RING_SHARE // 16
    first, second = mixed[:cut], mixed[cut:]
    whole_second = lax.all_gather(second, "tensor", axis=1, tiled=True)
    whole_first = jnp.zeros((cut, parts * local_width), BF16)
    for index, piece in ring_pieces(first, rights):
        whole_first = lax.dynamic_update_slice_in_dim(
            whole_first, piece, index * local_width, axis=1
        )
    units_first = active_units(whole_first)
    whole_second, units_first = lax.optimization_barrier((whole_second, units_first))

    def down_rows(index):
        weight = lax.dynamic_slice_in_dim(down_full, index * local_width, local_width, axis=0)
        return project_down(units_first, weight)

    sum_first, _ = ring_sum(down_rows, rights - 1)
    units_second = active_units(whole_second)
    sum_second = lax.psum_scatter(
        project_down(units_second, down_full), "tensor", scatter_dimension=1, tiled=True
    )
    return jnp.concatenate(
        [
            (first.astype(F32) + sum_first).astype(BF16),
            (second.astype(F32) + sum_second.astype(F32)).astype(BF16),
        ],
        axis=0,
    )


def solution(mesh):
    return jax.shard_map(
        shards,
        mesh=mesh,
        in_specs=(
            P("expert", "tensor"),
            P("expert", None),
            P("expert", None),
            P("expert", "tensor", None),
            P("expert", None, "tensor"),
            P(),
            P("expert", "tensor"),
            P("expert", "tensor"),
        ),
        out_specs=P("expert", "tensor"),
        check_vma=False,
    )
```

```python
import jax
import jax.numpy as jnp
from jax import lax
from jax.sharding import PartitionSpec as P

EXP_DEV = 2
F32 = jnp.float32
BF16 = jnp.bfloat16


def slot_rows(expert_col):
    expert = expert_col[:, 0]
    order = jnp.arange(expert.shape[0], dtype=jnp.int32)
    same = (expert[:, None] == expert[None, :]) & (order[None, :] < order[:, None])
    position = jnp.sum(same.astype(jnp.int32), axis=1)
    return expert, position


def trade(buffer):
    return lax.all_to_all(buffer, "expert", split_axis=0, concat_axis=0, tiled=True)


def hop(value, shift):
    n = lax.axis_size("tensor")
    return lax.ppermute(value, "tensor", [(i, (i + shift) % n) for i in range(n)])


def held(values, first):
    tied = lax.optimization_barrier((*values, *first))
    return list(tied[: len(values)])


def ring_sum(chunk, rights, ties=None):
    n = lax.axis_size("tensor")
    me = lax.axis_index("tensor")
    ways = ((1, rights), (-1, n - 1 - rights))
    flows = [chunk((me + shift * hops) % n) for shift, hops in ways]
    marks = {}
    for k in range(1, max(hops for _, hops in ways) + 1):
        for i, (shift, hops) in enumerate(ways):
            if k <= hops:
                flows[i] = hop(flows[i], shift)
        marks[k] = flows[0]
        if ties and k in ties:
            flows = held(flows, ties[k])
        for i, (shift, hops) in enumerate(ways):
            if k < hops:
                rest = chunk((me + shift * (hops - k)) % n).astype(F32)
                flows[i] = (flows[i].astype(F32) + rest).astype(BF16)
    return flows[0].astype(F32) + flows[1].astype(F32) + chunk(me).astype(F32), marks


def ring_pieces(own, rights, ties=None):
    n = lax.axis_size("tensor")
    me = lax.axis_index("tensor")
    pieces = [(me, own)]
    marks = {}
    right = left = own
    for k in range(1, n):
        if k <= rights:
            right = marks[k] = hop(right, 1)
        if k <= n - 1 - rights:
            left = hop(left, -1)
        if ties and k in ties:
            right, left = held((right, left), ties[k])
        if k <= rights:
            pieces.append(((me - k) % n, right))
        if k <= n - 1 - rights:
            pieces.append(((me + k) % n, left))
    return pieces, marks


def shards(tokens, expert_ids, gates, expert_in, expert_out, norm_gain, up_weight, down_weight):
    token_count, local_width = tokens.shape
    groups = lax.axis_size("expert")
    parts = lax.axis_size("tensor")
    experts = EXP_DEV * groups
    capacity = 2 * token_count // experts
    rows = groups * capacity
    expert, position = slot_rows(expert_ids)

    up_full = lax.all_gather(up_weight, "expert", axis=0, tiled=True)
    down_full = lax.all_gather(down_weight, "expert", axis=0, tiled=True)

    step = rows // parts
    rights = parts // 2
    selectors = []
    arrivals = []
    for j in range(EXP_DEV):
        row = jnp.where(expert % EXP_DEV == j, (expert // EXP_DEV) * capacity + position, -1)
        selector = (jnp.arange(rows, dtype=jnp.int32)[:, None] == row[None, :]).astype(BF16)
        outgoing = jnp.dot(selector, tokens, preferred_element_type=F32).astype(BF16)
        selectors.append(selector)
        arrivals.append(
            trade(outgoing.reshape(groups, capacity, local_width)).reshape(rows, local_width)
        )

    def hidden_rows(j):
        partial = jnp.dot(arrivals[j], expert_in[j], preferred_element_type=F32).astype(BF16)
        return lambda index: lax.dynamic_slice_in_dim(partial, index * step, step, axis=0)

    def place(pieces):
        active = jnp.zeros((rows, pieces[0][1].shape[1]), BF16)
        for index, piece in pieces:
            active = lax.dynamic_update_slice_in_dim(active, piece, index * step, axis=0)
        return active

    sum_first, marks = ring_sum(hidden_rows(0), rights, {1: arrivals[1:]})
    own_first = jax.nn.relu(sum_first).astype(BF16)
    pieces_first, marks_gather = ring_pieces(own_first, rights)
    sum_second, _ = ring_sum(
        hidden_rows(1),
        rights - 1,
        {1: [marks[3]], 2: [own_first], 3: [marks_gather[1]], 4: [marks_gather[2]]},
    )
    own_second = jax.nn.relu(sum_second).astype(BF16)
    active_first = place(pieces_first)
    pieces_second, _ = ring_pieces(
        own_second, rights - 1, {1: [marks_gather[3]], 2: [active_first]}
    )
    active_second = place(pieces_second)

    routed = jnp.zeros((token_count, local_width), F32)
    for j, active in enumerate((active_first, active_second)):
        produced = jnp.dot(active, expert_out[j], preferred_element_type=F32).astype(BF16)
        returned = trade(produced.reshape(groups, capacity, local_width)).reshape(rows, local_width)
        routed = routed + lax.dot_general(
            selectors[j], returned, (((0,), (0,)), ((), ())), preferred_element_type=F32
        )
    mixed = (tokens.astype(F32) + gates * routed).astype(BF16)

    half = token_count // 2
    me = lax.axis_index("tensor")

    def project_up(total, index, piece):
        hidden, squares = total
        wide = piece.astype(F32)
        gain = lax.dynamic_slice_in_dim(norm_gain, index * local_width, local_width, axis=0)
        weight = lax.dynamic_slice_in_dim(up_full, index * local_width, local_width, axis=0)
        hidden = hidden + jnp.dot((wide * gain).astype(BF16), weight, preferred_element_type=F32)
        return hidden, squares + jnp.sum(wide * wide, axis=1, keepdims=True)

    total = (
        jnp.zeros((token_count, up_full.shape[1]), F32),
        jnp.zeros((token_count, 1), F32),
    )
    ready = [(me, mixed)]
    right = left = mixed
    for k in range(1, parts // 2):
        right, left = hop(right, 1), hop(left, -1)
        for index, piece in ready:
            total = project_up(total, index, piece)
        right, left, *total = lax.optimization_barrier((right, left, *total))
        ready = [((me - k) % parts, right), ((me + k) % parts, left)]
    right, left = hop(right[:half], 1), hop(left[half:], -1)
    for index, piece in ready:
        total = project_up(total, index, piece)
    opposite = jnp.concatenate([right, left], axis=0)
    hidden, squares = project_up(total, (me + parts // 2) % parts, opposite)
    scale = lax.rsqrt(squares / (parts * local_width) + 1e-06)
    ffn_active = jax.nn.gelu(hidden * scale, approximate=True).astype(BF16)

    outputs = []
    for h in range(2):
        units = ffn_active[h * half : (h + 1) * half]

        def down_rows(index):
            weight = lax.dynamic_slice_in_dim(down_full, index * local_width, local_width, axis=0)
            return lax.dot_general(
                units, weight, (((1,), (1,)), ((), ())), preferred_element_type=F32
            ).astype(BF16)

        summed, _ = ring_sum(down_rows, parts // 2 - h)
        own = mixed[h * half : (h + 1) * half]
        outputs.append((own.astype(F32) + summed).astype(BF16))
    return jnp.concatenate(outputs, axis=0)


def solution(mesh):
    return jax.shard_map(
        shards,
        mesh=mesh,
        in_specs=(
            P("expert", "tensor"),
            P("expert", None),
            P("expert", None),
            P("expert", "tensor", None),
            P("expert", None, "tensor"),
            P(),
            P("expert", "tensor"),
            P("expert", "tensor"),
        ),
        out_specs=P("expert", "tensor"),
        check_vma=False,
    )
```

```python
import jax
import jax.numpy as jnp
from jax import lax
from jax.sharding import PartitionSpec as P

EXP_DEV = 2
F32 = jnp.float32
BF16 = jnp.bfloat16


def slot_rows(expert_col):
    expert = expert_col[:, 0]
    order = jnp.arange(expert.shape[0], dtype=jnp.int32)
    same = (expert[:, None] == expert[None, :]) & (order[None, :] < order[:, None])
    position = jnp.sum(same.astype(jnp.int32), axis=1)
    return expert, position


def trade(buffer):
    return lax.all_to_all(buffer, "expert", split_axis=0, concat_axis=0, tiled=True)


def hop(value, shift):
    n = lax.axis_size("tensor")
    return lax.ppermute(value, "tensor", [(i, (i + shift) % n) for i in range(n)])


def ring_sum(chunk, rights):
    n = lax.axis_size("tensor")
    flows = []
    for shift, hops in ((1, rights), (-1, n - 1 - rights)):
        total = chunk(shift * hops)
        for k in range(1, hops + 1):
            total = hop(total, shift).astype(F32)
            if k < hops:
                total = (total + chunk(shift * (hops - k)).astype(F32)).astype(BF16)
        flows.append(total)
    return flows[0] + flows[1] + chunk(0).astype(F32)


def ring_pieces(own, rights):
    n = lax.axis_size("tensor")
    me = lax.axis_index("tensor")
    pieces = [(me, own)]
    right = left = own
    for k in range(1, n):
        if k <= rights:
            right = hop(right, 1)
            pieces.append(((me - k) % n, right))
        if k <= n - 1 - rights:
            left = hop(left, -1)
            pieces.append(((me + k) % n, left))
    return pieces


def shards(tokens, expert_ids, gates, expert_in, expert_out, norm_gain, up_weight, down_weight):
    token_count, local_width = tokens.shape
    groups = lax.axis_size("expert")
    parts = lax.axis_size("tensor")
    experts = EXP_DEV * groups
    capacity = 2 * token_count // experts
    rows = groups * capacity
    me = lax.axis_index("tensor")
    expert, position = slot_rows(expert_ids)

    up_full = lax.all_gather(up_weight, "expert", axis=0, tiled=True)
    down_full = lax.all_gather(down_weight, "expert", axis=0, tiled=True)

    step = rows // parts
    rights = parts // 2
    row = expert * capacity + position
    selector = (jnp.arange(experts * capacity, dtype=jnp.int32)[:, None] == row[None, :]).astype(BF16)
    outgoing = jnp.dot(selector, tokens, preferred_element_type=F32).astype(BF16)
    arrived = trade(outgoing.reshape(groups, EXP_DEV, capacity, local_width))

    def place(pieces):
        active = jnp.zeros((rows, pieces[0][1].shape[1]), BF16)
        for index, piece in pieces:
            active = lax.dynamic_update_slice_in_dim(active, piece, index * step, axis=0)
        return active

    produced = []
    for j in range(EXP_DEV):
        partial = jnp.dot(
            arrived[:, j].reshape(rows, local_width), expert_in[j], preferred_element_type=F32
        ).astype(BF16)

        def hidden_rows(offset, partial=partial):
            start = (me + offset) % parts * step
            return lax.dynamic_slice_in_dim(partial, start, step, axis=0)

        own = jax.nn.relu(ring_sum(hidden_rows, rights - j)).astype(BF16)
        active = place(ring_pieces(own, rights - j))
        made = jnp.dot(active, expert_out[j], preferred_element_type=F32).astype(BF16)
        produced.append(made.reshape(groups, 1, capacity, local_width))
    returned = trade(jnp.concatenate(produced, axis=1)).reshape(experts * capacity, local_width)
    routed = lax.dot_general(
        selector, returned, (((0,), (0,)), ((), ())), preferred_element_type=F32
    )
    mixed = (tokens.astype(F32) + gates * routed).astype(BF16)

    half = token_count // 2
    def project_up(total, index, piece):
        hidden, squares = total
        wide = piece.astype(F32)
        gain = lax.dynamic_slice_in_dim(norm_gain, index * local_width, local_width, axis=0)
        weight = lax.dynamic_slice_in_dim(up_full, index * local_width, local_width, axis=0)
        hidden = hidden + jnp.dot((wide * gain).astype(BF16), weight, preferred_element_type=F32)
        return hidden, squares + jnp.sum(wide * wide, axis=1, keepdims=True)

    total = (
        jnp.zeros((token_count, up_full.shape[1]), F32),
        jnp.zeros((token_count, 1), F32),
    )
    ready = [(me, mixed)]
    right = left = mixed
    for k in range(1, parts // 2):
        right, left = hop(right, 1), hop(left, -1)
        for index, piece in ready:
            total = project_up(total, index, piece)
        right, left, *total = lax.optimization_barrier((right, left, *total))
        ready = [((me - k) % parts, right), ((me + k) % parts, left)]
    right, left = hop(right[:half], 1), hop(left[half:], -1)
    for index, piece in ready:
        total = project_up(total, index, piece)
    opposite = jnp.concatenate([right, left], axis=0)
    hidden, squares = project_up(total, (me + parts // 2) % parts, opposite)
    scale = lax.rsqrt(squares / (parts * local_width) + 1e-06)
    ffn_active = jax.nn.gelu(hidden * scale, approximate=True).astype(BF16)

    pieces = {}

    def down_rows(h):
        def rows_of(index_from_me):
            key = index_from_me % parts
            if key not in pieces:
                start = (me + key) % parts * local_width
                weight = lax.dynamic_slice_in_dim(down_full, start, local_width, axis=0)
                pieces[key] = lax.dot_general(
                    ffn_active, weight, (((1,), (1,)), ((), ())), preferred_element_type=F32
                ).astype(BF16)
            return pieces[key][h * half : (h + 1) * half]

        return rows_of

    outputs = [
        (mixed[h * half : (h + 1) * half].astype(F32) + ring_sum(down_rows(h), parts // 2 - h))
        .astype(BF16)
        for h in range(2)
    ]
    return jnp.concatenate(outputs, axis=0)


def solution(mesh):
    return jax.shard_map(
        shards,
        mesh=mesh,
        in_specs=(
            P("expert", "tensor"),
            P("expert", None),
            P("expert", None),
            P("expert", "tensor", None),
            P("expert", None, "tensor"),
            P(),
            P("expert", "tensor"),
            P("expert", "tensor"),
        ),
        out_specs=P("expert", "tensor"),
        check_vma=False,
    )
```

```python
import jax
import jax.numpy as jnp
from jax import lax
from jax.sharding import PartitionSpec as P

EXP_DEV = 2
F32 = jnp.float32
BF16 = jnp.bfloat16


def slot_rows(expert_col):
    expert = expert_col[:, 0]
    order = jnp.arange(expert.shape[0], dtype=jnp.int32)
    same = (expert[:, None] == expert[None, :]) & (order[None, :] < order[:, None])
    position = jnp.sum(same.astype(jnp.int32), axis=1)
    return expert, position


def trade(buffer):
    return lax.all_to_all(buffer, "expert", split_axis=0, concat_axis=0, tiled=True)


def hop(value, shift):
    n = lax.axis_size("tensor")
    return lax.ppermute(value, "tensor", [(i, (i + shift) % n) for i in range(n)])


def ring_sum(chunk, rights):
    n = lax.axis_size("tensor")
    flows = []
    for shift, hops in ((1, rights), (-1, n - 1 - rights)):
        total = chunk(shift * hops)
        for k in range(1, hops + 1):
            total = hop(total, shift).astype(F32)
            if k < hops:
                total = (total + chunk(shift * (hops - k)).astype(F32)).astype(BF16)
        flows.append(total)
    return flows[0] + flows[1] + chunk(0).astype(F32)


def ring_pieces(own, rights):
    n = lax.axis_size("tensor")
    me = lax.axis_index("tensor")
    pieces = [(me, own)]
    right = left = own
    for k in range(1, n):
        if k <= rights:
            right = hop(right, 1)
            pieces.append(((me - k) % n, right))
        if k <= n - 1 - rights:
            left = hop(left, -1)
            pieces.append(((me + k) % n, left))
    return pieces


def shards(tokens, expert_ids, gates, expert_in, expert_out, norm_gain, up_weight, down_weight):
    token_count, local_width = tokens.shape
    groups = lax.axis_size("expert")
    parts = lax.axis_size("tensor")
    experts = EXP_DEV * groups
    capacity = 2 * token_count // experts
    rows = groups * capacity
    me = lax.axis_index("tensor")
    expert, position = slot_rows(expert_ids)

    step = rows // parts
    rights = parts // 2
    row = expert * capacity + position
    selector = (jnp.arange(experts * capacity, dtype=jnp.int32)[:, None] == row[None, :]).astype(BF16)
    outgoing = jnp.dot(selector, tokens, preferred_element_type=F32).astype(BF16)
    arrived = trade(outgoing.reshape(groups, EXP_DEV, capacity, local_width))
    arrived, up_weight, down_weight = lax.optimization_barrier((arrived, up_weight, down_weight))
    up_full = lax.all_gather(up_weight, "expert", axis=0, tiled=True)
    down_full = lax.all_gather(down_weight, "expert", axis=0, tiled=True)

    def place(pieces):
        active = jnp.zeros((rows, pieces[0][1].shape[1]), BF16)
        for index, piece in pieces:
            active = lax.dynamic_update_slice_in_dim(active, piece, index * step, axis=0)
        return active

    produced = []
    for j in range(EXP_DEV):
        partial = jnp.dot(
            arrived[:, j].reshape(rows, local_width), expert_in[j], preferred_element_type=F32
        ).astype(BF16)

        def hidden_rows(offset, partial=partial):
            start = (me + offset) % parts * step
            return lax.dynamic_slice_in_dim(partial, start, step, axis=0)

        own = jax.nn.relu(ring_sum(hidden_rows, rights - j)).astype(BF16)
        active = place(ring_pieces(own, rights - j))
        made = jnp.dot(active, expert_out[j], preferred_element_type=F32).astype(BF16)
        produced.append(made.reshape(groups, 1, capacity, local_width))
    returned = trade(jnp.concatenate(produced, axis=1)).reshape(experts * capacity, local_width)
    routed = lax.dot_general(
        selector, returned, (((0,), (0,)), ((), ())), preferred_element_type=F32
    )
    mixed = (tokens.astype(F32) + gates * routed).astype(BF16)

    half = token_count // 2
    def project_up(total, index, piece):
        hidden, squares = total
        wide = piece.astype(F32)
        gain = lax.dynamic_slice_in_dim(norm_gain, index * local_width, local_width, axis=0)
        weight = lax.dynamic_slice_in_dim(up_full, index * local_width, local_width, axis=0)
        hidden = hidden + jnp.dot((wide * gain).astype(BF16), weight, preferred_element_type=F32)
        return hidden, squares + jnp.sum(wide * wide, axis=1, keepdims=True)

    total = (
        jnp.zeros((token_count, up_full.shape[1]), F32),
        jnp.zeros((token_count, 1), F32),
    )
    rights_to = [mixed[:half], mixed[half:]]
    lefts_to = [mixed[:half], mixed[half:]]
    ready = [(me, mixed)]
    for k in range(1, parts // 2 + 1):
        last = k == parts // 2
        rights_to[0] = hop(rights_to[0], 1)
        if not last:
            lefts_to[0] = hop(lefts_to[0], -1)
            rights_to[1] = hop(rights_to[1], 1)
        lefts_to[1] = hop(lefts_to[1], -1)
        for i in range(2):
            if i < len(ready):
                index, piece = ready[i]
                if i == 1:
                    piece, rights_to[0], lefts_to[0] = lax.optimization_barrier(
                        (piece, rights_to[0], lefts_to[0])
                    )
                total = project_up(total, index, piece)
            if not last:
                rights_to[i], lefts_to[i], *total = lax.optimization_barrier(
                    (rights_to[i], lefts_to[i], *total)
                )
        ready = [
            ((me - k) % parts, jnp.concatenate(rights_to, axis=0)),
            ((me + k) % parts, jnp.concatenate(lefts_to, axis=0)),
        ]
    opposite = jnp.concatenate([rights_to[0], lefts_to[1]], axis=0)
    hidden, squares = project_up(total, (me + parts // 2) % parts, opposite)
    scale = lax.rsqrt(squares / (parts * local_width) + 1e-06)
    ffn_active = jax.nn.gelu(hidden * scale, approximate=True).astype(BF16)

    pieces = {}

    def down_rows(h):
        def rows_of(index_from_me):
            key = index_from_me % parts
            if key not in pieces:
                start = (me + key) % parts * local_width
                weight = lax.dynamic_slice_in_dim(down_full, start, local_width, axis=0)
                pieces[key] = lax.dot_general(
                    ffn_active, weight, (((1,), (1,)), ((), ())), preferred_element_type=F32
                ).astype(BF16)
            return pieces[key][h * half : (h + 1) * half]

        return rows_of

    outputs = [
        (mixed[h * half : (h + 1) * half].astype(F32) + ring_sum(down_rows(h), parts // 2 - h))
        .astype(BF16)
        for h in range(2)
    ]
    return jnp.concatenate(outputs, axis=0)


def solution(mesh):
    return jax.shard_map(
        shards,
        mesh=mesh,
        in_specs=(
            P("expert", "tensor"),
            P("expert", None),
            P("expert", None),
            P("expert", "tensor", None),
            P("expert", None, "tensor"),
            P(),
            P("expert", "tensor"),
            P("expert", "tensor"),
        ),
        out_specs=P("expert", "tensor"),
        check_vma=False,
    )
```

```python
import jax
import jax.numpy as jnp
from jax import lax
from jax.sharding import PartitionSpec as P

EXP_DEV = 2
F32 = jnp.float32
BF16 = jnp.bfloat16


def slot_rows(expert_col):
    expert = expert_col[:, 0]
    order = jnp.arange(expert.shape[0], dtype=jnp.int32)
    same = (expert[:, None] == expert[None, :]) & (order[None, :] < order[:, None])
    position = jnp.sum(same.astype(jnp.int32), axis=1)
    return expert, position


def trade(buffer):
    return lax.all_to_all(buffer, "expert", split_axis=0, concat_axis=0, tiled=True)


def hop(value):
    groups, n = lax.axis_size("expert"), lax.axis_size("tensor")
    pairs = [
        (e * n + i, e * n + (i + (1 if e % 2 == 0 else n - 1)) % n)
        for e in range(groups)
        for i in range(n)
    ]
    return lax.ppermute(value, ("expert", "tensor"), pairs)


def ring_sum(chunk):
    n = lax.axis_size("tensor")
    total = chunk(n - 1)
    for k in range(n - 2, -1, -1):
        total = hop(total).astype(F32) + chunk(k).astype(F32)
        if k > 0:
            total = total.astype(BF16)
    return total


def ring_pieces(own):
    pieces = [own]
    for _ in range(1, lax.axis_size("tensor")):
        pieces.append(hop(pieces[-1]))
    return pieces


def shards(tokens, expert_ids, gates, expert_in, expert_out, norm_gain, up_weight, down_weight):
    token_count, local_width = tokens.shape
    groups = lax.axis_size("expert")
    parts = lax.axis_size("tensor")
    experts = EXP_DEV * groups
    capacity = 2 * token_count // experts
    rows = groups * capacity
    me = lax.axis_index("tensor")
    ahead = 1 - 2 * (lax.axis_index("expert") % 2)

    def place_at(offset):
        return (me + ahead * offset + parts) % parts

    expert, position = slot_rows(expert_ids)

    up_full = lax.all_gather(up_weight, "expert", axis=0, tiled=True)
    down_full = lax.all_gather(down_weight, "expert", axis=0, tiled=True)

    step = rows // parts
    row = expert * capacity + position
    selector = (jnp.arange(experts * capacity, dtype=jnp.int32)[:, None] == row[None, :]).astype(BF16)
    outgoing = jnp.dot(selector, tokens, preferred_element_type=F32).astype(BF16)
    arrived = trade(outgoing.reshape(groups, EXP_DEV, capacity, local_width))

    def place(pieces):
        active = jnp.zeros((rows, pieces[0].shape[1]), BF16)
        for k, piece in enumerate(pieces):
            active = lax.dynamic_update_slice_in_dim(active, piece, place_at(-k) * step, axis=0)
        return active

    produced = []
    for j in range(EXP_DEV):
        partial = jnp.dot(
            arrived[:, j].reshape(rows, local_width), expert_in[j], preferred_element_type=F32
        ).astype(BF16)

        def hidden_rows(offset, partial=partial):
            return lax.dynamic_slice_in_dim(partial, place_at(offset) * step, step, axis=0)

        own = jax.nn.relu(ring_sum(hidden_rows)).astype(BF16)
        active = place(ring_pieces(own))
        made = jnp.dot(active, expert_out[j], preferred_element_type=F32).astype(BF16)
        produced.append(made.reshape(groups, 1, capacity, local_width))
    returned = trade(jnp.concatenate(produced, axis=1)).reshape(experts * capacity, local_width)
    routed = lax.dot_general(
        selector, returned, (((0,), (0,)), ((), ())), preferred_element_type=F32
    )
    mixed = (tokens.astype(F32) + gates * routed).astype(BF16)

    half = token_count // 2
    def project_up(total, index, piece):
        hidden, squares = total
        wide = piece.astype(F32)
        gain = lax.dynamic_slice_in_dim(norm_gain, index * local_width, local_width, axis=0)
        weight = lax.dynamic_slice_in_dim(up_full, index * local_width, local_width, axis=0)
        hidden = hidden + jnp.dot((wide * gain).astype(BF16), weight, preferred_element_type=F32)
        return hidden, squares + jnp.sum(wide * wide, axis=1, keepdims=True)

    total = (
        jnp.zeros((token_count, up_full.shape[1]), F32),
        jnp.zeros((token_count, 1), F32),
    )
    streams = [mixed[:half], mixed[half:]]
    piece = mixed
    for k in range(parts):
        if k + 1 < parts:
            streams = [hop(v) for v in streams]
        total = project_up(total, place_at(-k), piece)
        if k + 1 < parts:
            streams[0], streams[1], *total = lax.optimization_barrier((*streams, *total))
            piece = jnp.concatenate(streams, axis=0)
    hidden, squares = total
    scale = lax.rsqrt(squares / (parts * local_width) + 1e-06)
    ffn_active = jax.nn.gelu(hidden * scale, approximate=True).astype(BF16)

    pieces = {}

    def down_rows(h):
        def rows_of(k):
            if k not in pieces:
                weight = lax.dynamic_slice_in_dim(
                    down_full, place_at(k) * local_width, local_width, axis=0
                )
                pieces[k] = lax.dot_general(
                    ffn_active, weight, (((1,), (1,)), ((), ())), preferred_element_type=F32
                ).astype(BF16)
            return pieces[k][h * half : (h + 1) * half]

        return rows_of

    outputs = [
        (mixed[h * half : (h + 1) * half].astype(F32) + ring_sum(down_rows(h))).astype(BF16)
        for h in range(2)
    ]
    return jnp.concatenate(outputs, axis=0)


def solution(mesh):
    return jax.shard_map(
        shards,
        mesh=mesh,
        in_specs=(
            P("expert", "tensor"),
            P("expert", None),
            P("expert", None),
            P("expert", "tensor", None),
            P("expert", None, "tensor"),
            P(),
            P("expert", "tensor"),
            P("expert", "tensor"),
        ),
        out_specs=P("expert", "tensor"),
        check_vma=False,
    )
```

```python
import jax
import jax.numpy as jnp
from jax import lax
from jax.sharding import PartitionSpec as P

EXP_DEV = 2
F32 = jnp.float32
BF16 = jnp.bfloat16


def slot_rows(expert_col):
    expert = expert_col[:, 0]
    order = jnp.arange(expert.shape[0], dtype=jnp.int32)
    same = (expert[:, None] == expert[None, :]) & (order[None, :] < order[:, None])
    position = jnp.sum(same.astype(jnp.int32), axis=1)
    return expert, position


def trade(buffer):
    return lax.all_to_all(buffer, "expert", split_axis=0, concat_axis=0, tiled=True)


def hop(value, shift):
    n = lax.axis_size("tensor")
    return lax.ppermute(value, "tensor", [(i, (i + shift) % n) for i in range(n)])


def ring_sum(chunk, rights):
    n = lax.axis_size("tensor")
    flows = []
    for shift, hops in ((1, rights), (-1, n - 1 - rights)):
        total = chunk(shift * hops)
        for k in range(1, hops + 1):
            total = hop(total, shift).astype(F32)
            if k < hops:
                total = (total + chunk(shift * (hops - k)).astype(F32)).astype(BF16)
        flows.append(total)
    return flows[0] + flows[1] + chunk(0).astype(F32)


def ring_pieces(own, rights):
    n = lax.axis_size("tensor")
    me = lax.axis_index("tensor")
    pieces = [(me, own)]
    right = left = own
    for k in range(1, n):
        if k <= rights:
            right = hop(right, 1)
            pieces.append(((me - k) % n, right))
        if k <= n - 1 - rights:
            left = hop(left, -1)
            pieces.append(((me + k) % n, left))
    return pieces


def shards(tokens, expert_ids, gates, expert_in, expert_out, norm_gain, up_weight, down_weight):
    token_count, local_width = tokens.shape
    groups = lax.axis_size("expert")
    parts = lax.axis_size("tensor")
    experts = EXP_DEV * groups
    capacity = 2 * token_count // experts
    rows = groups * capacity
    me = lax.axis_index("tensor")
    expert, position = slot_rows(expert_ids)

    up_full = lax.all_gather(up_weight, "expert", axis=0, tiled=True)
    down_full = lax.all_gather(down_weight, "expert", axis=0, tiled=True)

    step = rows // parts
    rights = parts // 2
    row = expert * capacity + position
    selector = (jnp.arange(experts * capacity, dtype=jnp.int32)[:, None] == row[None, :]).astype(BF16)
    outgoing = jnp.dot(selector, tokens, preferred_element_type=F32).astype(BF16)
    arrived = trade(outgoing.reshape(groups, EXP_DEV, capacity, local_width))

    def place(pieces):
        active = jnp.zeros((rows, pieces[0][1].shape[1]), BF16)
        for index, piece in pieces:
            active = lax.dynamic_update_slice_in_dim(active, piece, index * step, axis=0)
        return active

    produced = []
    for j in range(EXP_DEV):
        partial = jnp.dot(
            arrived[:, j].reshape(rows, local_width), expert_in[j], preferred_element_type=F32
        ).astype(BF16)

        def hidden_rows(offset, partial=partial):
            start = (me + offset) % parts * step
            return lax.dynamic_slice_in_dim(partial, start, step, axis=0)

        own = jax.nn.relu(ring_sum(hidden_rows, rights - j)).astype(BF16)
        active = place(ring_pieces(own, rights - j))
        made = jnp.dot(active, expert_out[j], preferred_element_type=F32).astype(BF16)
        produced.append(made.reshape(groups, 1, capacity, local_width))
    returned = trade(jnp.concatenate(produced, axis=1)).reshape(experts * capacity, local_width)
    routed = lax.dot_general(
        selector, returned, (((0,), (0,)), ((), ())), preferred_element_type=F32
    )
    mixed = (tokens.astype(F32) + gates * routed).astype(BF16)

    half = token_count // 2
    def project_up(total, index, piece):
        hidden, squares = total
        wide = piece.astype(F32)
        gain = lax.dynamic_slice_in_dim(norm_gain, index * local_width, local_width, axis=0)
        weight = lax.dynamic_slice_in_dim(up_full, index * local_width, local_width, axis=0)
        hidden = hidden + jnp.dot((wide * gain).astype(BF16), weight, preferred_element_type=F32)
        return hidden, squares + jnp.sum(wide * wide, axis=1, keepdims=True)

    total = (
        jnp.zeros((token_count, up_full.shape[1]), F32),
        jnp.zeros((token_count, 1), F32),
    )
    ready = [(me, mixed)]
    right = left = mixed
    for k in range(1, parts // 2):
        before = left
        right, left = hop(right, 1), hop(left, -1)
        for index, piece in ready:
            total = project_up(total, index, piece)
        right, before = lax.optimization_barrier((right, before))
        left, *total = lax.optimization_barrier((left, *total))
        ready = [((me - k) % parts, right), ((me + k) % parts, left)]
    right = hop(right, 1)
    ready.append(((me + parts // 2) % parts, right))
    for index, piece in ready:
        total = project_up(total, index, piece)
    hidden, squares = total
    scale = lax.rsqrt(squares / (parts * local_width) + 1e-06)
    ffn_active = jax.nn.gelu(hidden * scale, approximate=True).astype(BF16)

    pieces = {}

    def down_rows(h):
        def rows_of(index_from_me):
            key = index_from_me % parts
            if key not in pieces:
                start = (me + key) % parts * local_width
                weight = lax.dynamic_slice_in_dim(down_full, start, local_width, axis=0)
                pieces[key] = lax.dot_general(
                    ffn_active, weight, (((1,), (1,)), ((), ())), preferred_element_type=F32
                ).astype(BF16)
            return pieces[key][h * half : (h + 1) * half]

        return rows_of

    outputs = [
        (mixed[h * half : (h + 1) * half].astype(F32) + ring_sum(down_rows(h), parts // 2 - h))
        .astype(BF16)
        for h in range(2)
    ]
    return jnp.concatenate(outputs, axis=0)


def solution(mesh):
    return jax.shard_map(
        shards,
        mesh=mesh,
        in_specs=(
            P("expert", "tensor"),
            P("expert", None),
            P("expert", None),
            P("expert", "tensor", None),
            P("expert", None, "tensor"),
            P(),
            P("expert", "tensor"),
            P("expert", "tensor"),
        ),
        out_specs=P("expert", "tensor"),
        check_vma=False,
    )
```

```python
import jax
import jax.numpy as jnp
from jax import lax
from jax.sharding import PartitionSpec as P

EXP_DEV = 2
F32 = jnp.float32
BF16 = jnp.bfloat16


def slot_rows(expert_col):
    expert = expert_col[:, 0]
    order = jnp.arange(expert.shape[0], dtype=jnp.int32)
    same = (expert[:, None] == expert[None, :]) & (order[None, :] < order[:, None])
    position = jnp.sum(same.astype(jnp.int32), axis=1)
    return expert, position


def trade(buffer):
    return lax.all_to_all(buffer, "expert", split_axis=0, concat_axis=0, tiled=True)


def hop(value, shift):
    n = lax.axis_size("tensor")
    return lax.ppermute(value, "tensor", [(i, (i + shift) % n) for i in range(n)])


def ring_sum(chunk, rights):
    n = lax.axis_size("tensor")
    flows = []
    for shift, hops in ((1, rights), (-1, n - 1 - rights)):
        total = chunk(shift * hops)
        for k in range(1, hops + 1):
            total = hop(total, shift).astype(F32)
            if k < hops:
                total = (total + chunk(shift * (hops - k)).astype(F32)).astype(BF16)
        flows.append(total)
    return flows[0] + flows[1] + chunk(0).astype(F32)


def ring_pieces(own, rights):
    n = lax.axis_size("tensor")
    me = lax.axis_index("tensor")
    pieces = [(me, own)]
    right = left = own
    for k in range(1, n):
        if k <= rights:
            right = hop(right, 1)
            pieces.append(((me - k) % n, right))
        if k <= n - 1 - rights:
            left = hop(left, -1)
            pieces.append(((me + k) % n, left))
    return pieces


def shards(tokens, expert_ids, gates, expert_in, expert_out, norm_gain, up_weight, down_weight):
    token_count, local_width = tokens.shape
    groups = lax.axis_size("expert")
    parts = lax.axis_size("tensor")
    experts = EXP_DEV * groups
    capacity = 2 * token_count // experts
    rows = groups * capacity
    me = lax.axis_index("tensor")
    expert, position = slot_rows(expert_ids)

    step = rows // parts
    rights = parts // 2
    row = expert * capacity + position
    selector = (jnp.arange(experts * capacity, dtype=jnp.int32)[:, None] == row[None, :]).astype(BF16)
    outgoing = jnp.dot(selector, tokens, preferred_element_type=F32).astype(BF16)
    arrived = trade(outgoing.reshape(groups, EXP_DEV, capacity, local_width))
    both = jnp.stack([up_weight, down_weight])
    arrived, both = lax.optimization_barrier((arrived, both))
    gathered = lax.all_gather(both, "expert", axis=0)
    blocks = local_width // up_weight.shape[0]

    def weight_rows(which, index):
        part = lax.dynamic_slice_in_dim(gathered, index * blocks, blocks, axis=0)[:, which]
        return part.reshape(local_width, -1)

    def place(pieces):
        active = jnp.zeros((rows, pieces[0][1].shape[1]), BF16)
        for index, piece in pieces:
            active = lax.dynamic_update_slice_in_dim(active, piece, index * step, axis=0)
        return active

    produced = []
    for j in range(EXP_DEV):
        partial = jnp.dot(
            arrived[:, j].reshape(rows, local_width), expert_in[j], preferred_element_type=F32
        ).astype(BF16)

        def hidden_rows(offset, partial=partial):
            start = (me + offset) % parts * step
            return lax.dynamic_slice_in_dim(partial, start, step, axis=0)

        own = jax.nn.relu(ring_sum(hidden_rows, rights - j)).astype(BF16)
        active = place(ring_pieces(own, rights - j))
        made = jnp.dot(active, expert_out[j], preferred_element_type=F32).astype(BF16)
        produced.append(made.reshape(groups, 1, capacity, local_width))
    returned = trade(jnp.concatenate(produced, axis=1)).reshape(experts * capacity, local_width)
    routed = lax.dot_general(
        selector, returned, (((0,), (0,)), ((), ())), preferred_element_type=F32
    )
    mixed = (tokens.astype(F32) + gates * routed).astype(BF16)

    half = token_count // 2
    def project_up(total, index, piece):
        hidden, squares = total
        wide = piece.astype(F32)
        gain = lax.dynamic_slice_in_dim(norm_gain, index * local_width, local_width, axis=0)
        weight = weight_rows(0, index)
        hidden = hidden + jnp.dot((wide * gain).astype(BF16), weight, preferred_element_type=F32)
        return hidden, squares + jnp.sum(wide * wide, axis=1, keepdims=True)

    total = (
        jnp.zeros((token_count, up_weight.shape[1]), F32),
        jnp.zeros((token_count, 1), F32),
    )
    ready = [(me, mixed)]
    right = left = mixed
    for k in range(1, parts // 2):
        right, left = hop(right, 1), hop(left, -1)
        for index, piece in ready:
            total = project_up(total, index, piece)
        right, left, *total = lax.optimization_barrier((right, left, *total))
        ready = [((me - k) % parts, right), ((me + k) % parts, left)]
    right, left = hop(right[:half], 1), hop(left[half:], -1)
    for index, piece in ready:
        total = project_up(total, index, piece)
    opposite = jnp.concatenate([right, left], axis=0)
    hidden, squares = project_up(total, (me + parts // 2) % parts, opposite)
    scale = lax.rsqrt(squares / (parts * local_width) + 1e-06)
    ffn_active = jax.nn.gelu(hidden * scale, approximate=True).astype(BF16)

    pieces = {}

    def down_rows(h):
        def rows_of(index_from_me):
            key = index_from_me % parts
            if key not in pieces:
                weight = weight_rows(1, (me + key) % parts)
                pieces[key] = lax.dot_general(
                    ffn_active, weight, (((1,), (1,)), ((), ())), preferred_element_type=F32
                ).astype(BF16)
            return pieces[key][h * half : (h + 1) * half]

        return rows_of

    outputs = [
        (mixed[h * half : (h + 1) * half].astype(F32) + ring_sum(down_rows(h), parts // 2 - h))
        .astype(BF16)
        for h in range(2)
    ]
    return jnp.concatenate(outputs, axis=0)


def solution(mesh):
    return jax.shard_map(
        shards,
        mesh=mesh,
        in_specs=(
            P("expert", "tensor"),
            P("expert", None),
            P("expert", None),
            P("expert", "tensor", None),
            P("expert", None, "tensor"),
            P(),
            P("expert", "tensor"),
            P("expert", "tensor"),
        ),
        out_specs=P("expert", "tensor"),
        check_vma=False,
    )
```

```python
import jax
import jax.numpy as jnp
from jax import lax
from jax.sharding import PartitionSpec as P

EXP_DEV = 2
F32 = jnp.float32
BF16 = jnp.bfloat16


def slot_rows(expert_col):
    expert = expert_col[:, 0]
    order = jnp.arange(expert.shape[0], dtype=jnp.int32)
    same = (expert[:, None] == expert[None, :]) & (order[None, :] < order[:, None])
    position = jnp.sum(same.astype(jnp.int32), axis=1)
    return expert, position


def trade(buffer):
    return lax.all_to_all(buffer, "expert", split_axis=0, concat_axis=0, tiled=True)


def hop(value, shift):
    n = lax.axis_size("tensor")
    return lax.ppermute(value, "tensor", [(i, (i + shift) % n) for i in range(n)])


def ring_sum(chunk, rights):
    n = lax.axis_size("tensor")
    flows = []
    for shift, hops in ((1, rights), (-1, n - 1 - rights)):
        total = chunk(shift * hops)
        for k in range(1, hops + 1):
            total = hop(total, shift).astype(F32)
            if k < hops:
                total = (total + chunk(shift * (hops - k)).astype(F32)).astype(BF16)
        flows.append(total)
    return flows[0] + flows[1] + chunk(0).astype(F32)


def ring_pieces(own, rights):
    n = lax.axis_size("tensor")
    me = lax.axis_index("tensor")
    pieces = [(me, own)]
    right = left = own
    for k in range(1, n):
        if k <= rights:
            right = hop(right, 1)
            pieces.append(((me - k) % n, right))
        if k <= n - 1 - rights:
            left = hop(left, -1)
            pieces.append(((me + k) % n, left))
    return pieces


def shards(tokens, expert_ids, gates, expert_in, expert_out, norm_gain, up_weight, down_weight):
    token_count, local_width = tokens.shape
    groups = lax.axis_size("expert")
    parts = lax.axis_size("tensor")
    experts = EXP_DEV * groups
    capacity = 2 * token_count // experts
    rows = groups * capacity
    me = lax.axis_index("tensor")
    expert, position = slot_rows(expert_ids)

    step = rows // parts
    rights = parts // 2
    row = expert * capacity + position
    selector = (jnp.arange(experts * capacity, dtype=jnp.int32)[:, None] == row[None, :]).astype(BF16)
    outgoing = jnp.dot(selector, tokens, preferred_element_type=F32).astype(BF16)
    arrived = trade(outgoing.reshape(groups, EXP_DEV, capacity, local_width))
    both = jnp.stack([up_weight, down_weight])
    arrived, both = lax.optimization_barrier((arrived, both))
    gathered = lax.all_gather(both, "expert", axis=0)
    blocks = local_width // up_weight.shape[0]

    def weight_rows(which, index):
        part = lax.dynamic_slice_in_dim(gathered, index * blocks, blocks, axis=0)[:, which]
        return part.reshape(local_width, -1)

    def place(pieces):
        active = jnp.zeros((rows, pieces[0][1].shape[1]), BF16)
        for index, piece in pieces:
            active = lax.dynamic_update_slice_in_dim(active, piece, index * step, axis=0)
        return active

    produced = []
    for j in range(EXP_DEV):
        partial = jnp.dot(
            arrived[:, j].reshape(rows, local_width), expert_in[j], preferred_element_type=F32
        ).astype(BF16)

        def hidden_rows(offset, partial=partial):
            start = (me + offset) % parts * step
            return lax.dynamic_slice_in_dim(partial, start, step, axis=0)

        own = jax.nn.relu(ring_sum(hidden_rows, rights)).astype(BF16)
        active = place(ring_pieces(own, rights))
        made = jnp.dot(active, expert_out[j], preferred_element_type=F32).astype(BF16)
        produced.append(made.reshape(groups, 1, capacity, local_width))
    returned = trade(jnp.concatenate(produced, axis=1)).reshape(experts * capacity, local_width)
    routed = lax.dot_general(
        selector, returned, (((0,), (0,)), ((), ())), preferred_element_type=F32
    )
    mixed = (tokens.astype(F32) + gates * routed).astype(BF16)

    half = token_count // 2
    def project_up(total, index, piece):
        hidden, squares = total
        wide = piece.astype(F32)
        gain = lax.dynamic_slice_in_dim(norm_gain, index * local_width, local_width, axis=0)
        weight = weight_rows(0, index)
        hidden = hidden + jnp.dot((wide * gain).astype(BF16), weight, preferred_element_type=F32)
        return hidden, squares + jnp.sum(wide * wide, axis=1, keepdims=True)

    total = (
        jnp.zeros((token_count, up_weight.shape[1]), F32),
        jnp.zeros((token_count, 1), F32),
    )
    ready = [(me, mixed)]
    right = left = mixed
    for k in range(1, parts // 2):
        right, left = hop(right, 1), hop(left, -1)
        for index, piece in ready:
            total = project_up(total, index, piece)
        right, left, *total = lax.optimization_barrier((right, left, *total))
        ready = [((me - k) % parts, right), ((me + k) % parts, left)]
    right, left = hop(right[:half], 1), hop(left[half:], -1)
    for index, piece in ready:
        total = project_up(total, index, piece)
    opposite = jnp.concatenate([right, left], axis=0)
    hidden, squares = project_up(total, (me + parts // 2) % parts, opposite)
    scale = lax.rsqrt(squares / (parts * local_width) + 1e-06)
    ffn_active = jax.nn.gelu(hidden * scale, approximate=True).astype(BF16)

    pieces = {}

    def down_rows(h):
        def rows_of(index_from_me):
            key = index_from_me % parts
            if key not in pieces:
                weight = weight_rows(1, (me + key) % parts)
                pieces[key] = lax.dot_general(
                    ffn_active, weight, (((1,), (1,)), ((), ())), preferred_element_type=F32
                ).astype(BF16)
            return pieces[key][h * half : (h + 1) * half]

        return rows_of

    outputs = [
        (mixed[h * half : (h + 1) * half].astype(F32) + ring_sum(down_rows(h), parts // 2 - h))
        .astype(BF16)
        for h in range(2)
    ]
    return jnp.concatenate(outputs, axis=0)


def solution(mesh):
    return jax.shard_map(
        shards,
        mesh=mesh,
        in_specs=(
            P("expert", "tensor"),
            P("expert", None),
            P("expert", None),
            P("expert", "tensor", None),
            P("expert", None, "tensor"),
            P(),
            P("expert", "tensor"),
            P("expert", "tensor"),
        ),
        out_specs=P("expert", "tensor"),
        check_vma=False,
    )
```
